256 devices in a mesh: depth: 4 (over x_lo, core), row: 8 (over y, x_hi), col: 8 (over z).
Axes of the slice: x: 4 (x_hi: 2, x_lo: 2; x = x_hi * 2 + x_lo), y: 4, z: 8, core: 2. Of those that a mesh axis runs over, the one named last changes fastest.
Arguments:
- tokens: bfloat16 [16384, 2560], P(('depth', 'row'), 'col'), may hold values from -6 to 6
- up_weight: bfloat16 [2560, 10240], P('row', 'col'), may hold values from -0.125 to 0.125
- upstream: bfloat16 [16384, 10240], P(('depth', 'row'), 'col'), may hold values from -6 to 6
Outputs:
- activated: bfloat16 [16384, 10240], P(('depth', 'row'), 'col')
- input_grad: bfloat16 [16384, 2560], P(('depth', 'row'), 'col')
- weight_grad: float32 [2560, 10240], P('row', 'col')
The draws below stay inside these ranges and needn't reach their ends.
All inputs are finite; a program needn't handle non-finite values.
Results may differ from the reference program's by a relative error of at most 0.0049.
Values may be sent and summed in bfloat16 or wider, within the bound.
No kernel may reach another device: no remote copies, remote signals or barrier semaphores. Data moves between devices by JAX's collectives and lax.ppermute only.
A program may use at most 128 MiB of HBM per device.

```python
import math
import jax
import jax.numpy as jnp

D = 2560
FF = 10240
TOKENS = 16384


def with_spikes(result, key, source, target, shards_of, factor):
    owner, partner = [(jnp.arange(result.shape[position]) // (result.shape[position] // shards_of)).reshape([-1 if axis == position else 1 for axis in range(result.ndim)]) for position in (source, target)]
    chosen = jax.random.permutation(key, shards_of)[partner]
    strong = (owner == chosen) | (owner == (partner + shards_of // 2) % shards_of)
    return jnp.where(strong, factor * result, result)


def level_of(stream_key, shape, split, least, high):
    level, own = 1.0, jax.random.fold_in(stream_key, 6)
    for axis_at, parts in split:
        heights = jnp.exp(jax.random.uniform(jax.random.fold_in(own, axis_at), (parts,), jnp.float32, least / len(split), high / len(split)))
        level = level * jnp.repeat(heights, shape[axis_at] // parts).reshape([-1 if axis == axis_at else 1 for axis in range(len(shape))])
    return level


def gaussian(key, dims, spread, bound, pieces=(), kind=jnp.bfloat16):
    drawn = spread * jax.random.normal(key, dims, jnp.float32)
    if pieces:
        drawn = drawn * level_of(key, dims, pieces, -0.22, 0.18)
    return jnp.clip(drawn, -bound, bound).astype(kind)


def noise_with(own_key, shape, scale, limit, cuts, heavy, kind=jnp.bfloat16):
    drawn = scale * jax.random.normal(own_key, shape, jnp.float32)
    if cuts:
        drawn = drawn * level_of(own_key, shape, cuts, -0.22, 0.18)
    return jnp.clip(with_spikes(drawn, jax.random.fold_in(own_key, 3), *heavy), -limit, limit).astype(kind)


def setup_inputs(seed: int = 0) -> dict:
    seeds = jax.random.split(jax.random.key(seed), 4)
    return {
        "tokens": noise_with(seeds[0], (TOKENS, D), 1.0, 6.0, ((0, 32), (1, 8)), (0, 1, 32, 2.75)),
        "up_weight": gaussian(seeds[1], (D, FF), D ** -0.5, 0.125, ((0, 8), (1, 8))),
        "upstream": gaussian(seeds[2], (TOKENS, FF), 1.0, 6.0, ((0, 32), (1, 8))),
    }


def gelu_parts(pre):
    coeff = 0.7978845608
    cube = 0.044715
    inner = coeff * (pre + cube * pre * pre * pre)
    tangent = jnp.tanh(inner)
    value = 0.5 * pre * (1.0 + tangent)
    slope = 0.5 * (1.0 + tangent) + 0.5 * pre * (1.0 - tangent * tangent) * coeff * (1.0 + 3.0 * cube * pre * pre)
    return (value, slope)

def reference(tokens, up_weight, upstream):
    hidden_pre = jnp.dot(tokens, up_weight, preferred_element_type=jnp.float32)
    value, slope = gelu_parts(hidden_pre)
    activated = value.astype(jnp.bfloat16)
    scaled = (upstream.astype(jnp.float32) * slope).astype(jnp.bfloat16)
    input_grad = jnp.dot(scaled, up_weight.T, preferred_element_type=jnp.float32).astype(jnp.bfloat16)
    weight_grad = jnp.dot(tokens.T, scaled, preferred_element_type=jnp.float32) * (1.0 / math.sqrt(TOKENS))
    return (activated, input_grad, weight_grad)
```

```python
import math

import jax
import jax.numpy as jnp
from jax import lax
from jax.experimental import pallas as pl
from jax.experimental.pallas import tpu as pltpu
from jax.sharding import PartitionSpec as P

AXES = ("depth", "row", "col")
BF = jnp.bfloat16
F32 = jnp.float32
VM = pl.BlockSpec(memory_space=pltpu.VMEM)
LIMIT = 56 * 1024 * 1024


def gelu_parts(pre):
    coeff = 0.7978845608
    cube = 0.044715
    inner = coeff * (pre + cube * pre * pre * pre)
    tangent = jnp.tanh(inner)
    value = 0.5 * pre * (1.0 + tangent)
    slope = 0.5 * (1.0 + tangent) + 0.5 * pre * (1.0 - tangent * tangent) * coeff * (
        1.0 + 3.0 * cube * pre * pre
    )
    return (value, slope)


def place():
    return lax.axis_index("depth") % 2, lax.axis_index("row") // 2, lax.axis_index("row") % 2


def move(x, target):
    n_depth, n_row, n_col = (lax.axis_size(a) for a in AXES)
    pairs = []
    for d in range(n_depth):
        for r in range(n_row):
            for z in range(n_col):
                xl, c, y, xh, w = target(d // 2, d % 2, r // 2, r % 2, z)
                to = ((xl * 2 + c) * n_row + y * 2 + xh) * n_col + w
                pairs.append(((d * n_row + r) * n_col + z, to))
    return lax.ppermute(x, AXES, pairs)


def up(x):
    return move(x, lambda xl, c, y, xh, z: (xl, c, (y + 1) % 4, xh, z))


def down(x):
    return move(x, lambda xl, c, y, xh, z: (xl, c, (y + 3) % 4, xh, z))


def across(x):
    return move(x, lambda xl, c, y, xh, z: (1 - xl, c, y, 1 - xh, z))


def beside(x):
    return move(x, lambda xl, c, y, xh, z: (1 - xl, c, y, xh, z))


def sibling(x):
    return move(x, lambda xl, c, y, xh, z: (xl, 1 - c, y, xh, z))


def row_block(s, k):
    _, y, xh = place()
    other = xh if s == 0 else 1 - xh
    return pl.multiple_of((((y + k) % 4) * 2 + other) * 320, 64)


def forward_kernel(tok, wom, wxm, wos, wxs, ups, act, scal_m, scal_o, tokr, wide):
    c, _, _ = place()
    half = wom.shape[1]
    side = wom.shape[0]
    for s in range(2):
        for k in range(4):
            tokr[pl.ds(s * side + k * 320, 320), :] = tok[pl.ds(row_block(s, k), 320), :]
    wide[...] = tokr[...].T
    rows = 128
    for mine, wo, wx, out in ((False, wos, wxs, scal_o), (True, wom, wxm, scal_m)):
        col = pl.multiple_of((c if mine else 1 - c) * half, 128)

        def body(i, _):
            at = pl.ds(pl.multiple_of(i * rows, rows), rows)
            pre = jnp.dot(wide[at, :side], wo[...], preferred_element_type=F32)
            pre = pre + jnp.dot(wide[at, side:], wx[...], preferred_element_type=F32)
            value, slope = gelu_parts(pre)
            act[at, pl.ds(col, half)] = value.astype(BF)
            out[at, :] = (ups[at, pl.ds(col, half)].astype(F32) * slope).astype(BF)
            return 0

        lax.fori_loop(0, wide.shape[0] // rows, body, 0)


def forward(tok, wom, wxm, wos, wxs, ups):
    n_feat, n_tok = tok.shape
    half = wom.shape[1]
    return pl.pallas_call(
        forward_kernel,
        out_shape=(
            jax.ShapeDtypeStruct(ups.shape, BF),
            jax.ShapeDtypeStruct((n_tok, half), BF),
            jax.ShapeDtypeStruct((n_tok, half), BF),
        ),
        in_specs=[VM] * 6,
        out_specs=(VM,) * 3,
        scratch_shapes=[pltpu.VMEM((n_feat, n_tok), BF), pltpu.VMEM((n_tok, n_feat), BF)],
        compiler_params=pltpu.CompilerParams(vmem_limit_bytes=LIMIT),
        cost_estimate=pl.CostEstimate(
            flops=4 * n_feat * n_tok * half, bytes_accessed=14 << 20, transcendentals=2 * n_tok * half
        ),
        name="forward",
    )(tok, wom, wxm, wos, wxs, ups)


def input_kernel(wom, wxm, wos, wxs, scal_m, scal_o, out):
    dims = (((1,), (1,)), ((), ()))
    for s, wm, ws in ((0, wom, wos), (1, wxm, wxs)):
        for k in range(4):
            at = pl.ds(k * 320, 320)
            part = lax.dot_general(wm[at, :], scal_m[...], dims, preferred_element_type=F32)
            part = part + lax.dot_general(ws[at, :], scal_o[...], dims, preferred_element_type=F32)
            out[pl.ds(row_block(s, k), 320), :] = part.astype(BF)


def input_partial(wom, wxm, wos, wxs, scal_m, scal_o):
    n_tok = scal_m.shape[0]
    n_feat = 2 * wom.shape[0]
    return pl.pallas_call(
        input_kernel,
        out_shape=jax.ShapeDtypeStruct((n_feat, n_tok), BF),
        in_specs=[VM] * 6,
        out_specs=VM,
        compiler_params=pltpu.CompilerParams(vmem_limit_bytes=LIMIT),
        cost_estimate=pl.CostEstimate(
            flops=4 * n_feat * n_tok * scal_m.shape[1], bytes_accessed=11 << 20, transcendentals=0
        ),
        name="input_partial",
    )(wom, wxm, wos, wxs, scal_m, scal_o)


def weight_kernel(s, tok, tok_s, scal, scal_s, far_a, far_b, near_p, near_m, own):
    def block(k):
        at = pl.ds(row_block(s, k), 320)
        part = jnp.dot(tok[at, :], scal[...], preferred_element_type=F32)
        return part + jnp.dot(tok_s[at, :], scal_s[...], preferred_element_type=F32)

    far = block(2).astype(BF)
    far_a[...] = far[:160]
    far_b[...] = far[160:]
    near_p[...] = block(1).astype(BF)
    near_m[...] = block(3).astype(BF)
    own[...] = block(0)


def weight_partial(s, tok, tok_s, scal, scal_s):
    n_feat, n_tok = tok.shape
    half = scal.shape[1]
    shape = jax.ShapeDtypeStruct
    return pl.pallas_call(
        lambda *refs: weight_kernel(s, *refs),
        out_shape=(
            shape((160, half), BF),
            shape((160, half), BF),
            shape((320, half), BF),
            shape((320, half), BF),
            shape((320, half), F32),
        ),
        in_specs=[VM] * 4,
        out_specs=(VM,) * 5,
        compiler_params=pltpu.CompilerParams(vmem_limit_bytes=LIMIT),
        cost_estimate=pl.CostEstimate(
            flops=2 * n_feat * n_tok * half, bytes_accessed=9 << 20, transcendentals=0
        ),
        name="weight_partial",
    )(tok, tok_s, scal, scal_s)


def ring_gather(x):
    above = down(x)
    below = up(x)
    far_a = down(above[:160])
    far_b = up(below[160:])
    return jnp.concatenate([x, above, far_a, far_b, below], axis=0)


def ring_sum(far_a, far_b, near_p, near_m, own):
    got_a = up(far_a)
    got_b = down(far_b)
    first = (near_p[:160].astype(F32) + got_a.astype(F32)).astype(BF)
    second = (near_m[160:].astype(F32) + got_b.astype(F32)).astype(BF)
    from_below = up(jnp.concatenate([first, near_p[160:]], axis=0))
    from_above = down(jnp.concatenate([near_m[:160], second], axis=0))
    return own + from_below.astype(F32) + from_above.astype(F32)


def shards(tokens, up_weight, upstream):
    token_rows = tokens.shape[0]
    half = up_weight.shape[1] // 2
    c, _, _ = place()
    factor = 1.0 / math.sqrt(token_rows * lax.axis_size("depth") * lax.axis_size("row"))

    own_w = lax.dynamic_slice_in_dim(up_weight, c * half, half, axis=1)
    tok = lax.all_gather(tokens.T, "col", axis=0, tiled=True)
    cross_w = across(own_w)
    wom = ring_gather(own_w)
    wos = sibling(wom)
    wxm = ring_gather(cross_w)
    wxs = sibling(wxm)

    tok_s = sibling(tok)
    activated, scal_m, scal_o = forward(tok, wom, wxm, wos, wxs, upstream)
    scal_s = sibling(scal_o)
    grad_part = input_partial(wom, wxm, wos, wxs, scal_m, scal_o)
    grad_rows = lax.psum_scatter(grad_part, "col", scatter_dimension=0, tiled=True)
    input_grad = grad_rows.T

    to_cross = ring_sum(*weight_partial(1, tok, tok_s, scal_m, scal_s))
    from_cross = across(to_cross.astype(BF))
    kept = ring_sum(*weight_partial(0, tok, tok_s, scal_m, scal_s))
    summed = (kept + from_cross.astype(F32)).astype(BF)
    total = (summed.astype(F32) + beside(summed).astype(F32)) * factor
    total_s = sibling(total)
    weight_grad = jnp.where(
        c == 0,
        jnp.concatenate([total, total_s], axis=1),
        jnp.concatenate([total_s, total], axis=1),
    )
    return (activated, input_grad, weight_grad)


def solution(mesh):
    placed = (P(("depth", "row"), "col"), P("row", "col"), P(("depth", "row"), "col"))
    return jax.shard_map(
        shards,
        mesh=mesh,
        in_specs=placed,
        out_specs=(P(("depth", "row"), "col"), P(("depth", "row"), "col"), P("row", "col")),
        check_vma=False,
    )
```

```python
import math

import jax
import jax.numpy as jnp
from jax import lax
from jax.experimental import pallas as pl
from jax.experimental.pallas import tpu as pltpu
from jax.sharding import PartitionSpec as P

AXES = ("depth", "row", "col")
BF = jnp.bfloat16
F32 = jnp.float32
VM = pl.BlockSpec(memory_space=pltpu.VMEM)


def gelu_parts(pre):
    coeff = 0.7978845608
    cube = 0.044715
    inner = coeff * (pre + cube * pre * pre * pre)
    tangent = jnp.tanh(inner)
    value = 0.5 * pre * (1.0 + tangent)
    slope = 0.5 * (1.0 + tangent) + 0.5 * pre * (1.0 - tangent * tangent) * coeff * (
        1.0 + 3.0 * cube * pre * pre
    )
    return (value, slope)


def place():
    return lax.axis_index("depth") % 2, lax.axis_index("row") // 2, lax.axis_index("row") % 2


def move(x, target):
    n_depth, n_row, n_col = (lax.axis_size(a) for a in AXES)
    pairs = []
    for d in range(n_depth):
        for r in range(n_row):
            for z in range(n_col):
                xl, c, y, xh, w = target(d // 2, d % 2, r // 2, r % 2, z)
                to = ((xl * 2 + c) * n_row + y * 2 + xh) * n_col + w
                pairs.append(((d * n_row + r) * n_col + z, to))
    return lax.ppermute(x, AXES, pairs)


def up(x):
    return move(x, lambda xl, c, y, xh, z: (xl, c, (y + 1) % 4, xh, z))


def down(x):
    return move(x, lambda xl, c, y, xh, z: (xl, c, (y + 3) % 4, xh, z))


def opposite(x):
    return move(x, lambda xl, c, y, xh, z: (xl, c, (y + 2) % 4, xh, z))


def across(x):
    return move(x, lambda xl, c, y, xh, z: (1 - xl, c, y, 1 - xh, z))


def beside(x):
    return move(x, lambda xl, c, y, xh, z: (1 - xl, c, y, xh, z))


def sibling(x):
    return move(x, lambda xl, c, y, xh, z: (xl, 1 - c, y, xh, z))


def zup(x):
    return move(x, lambda xl, c, y, xh, z: (xl, c, y, xh, (z + 1) % 8))


def zdown(x):
    return move(x, lambda xl, c, y, xh, z: (xl, c, y, xh, (z + 7) % 8))


def row_block(s, k):
    _, y, xh = place()
    other = xh if s == 0 else 1 - xh
    block = ((y + k) % 4) * 2 + other
    return pl.multiple_of(((block + 8 - lax.axis_index("col")) % 8) * 320, 64)


def hidden_part(wide, wo, wx, ups, col, put_act, put_scal):
    side, half = wo.shape
    rows = 128

    def body(i, _):
        at = pl.ds(pl.multiple_of(i * rows, rows), rows)
        pre = jnp.dot(wide[at, :side], wo[...], preferred_element_type=F32)
        pre = pre + jnp.dot(wide[at, side:], wx[...], preferred_element_type=F32)
        value, slope = gelu_parts(pre)
        put_act(at, value.astype(BF))
        put_scal[at, :] = (ups[at, pl.ds(col, half)].astype(F32) * slope).astype(BF)
        return 0

    lax.fori_loop(0, wide.shape[0] // rows, body, 0)


def first_kernel(tok, wom, wxm, ups, wide, act_m, scal_m, tokr):
    side, half = wom.shape
    for s in range(2):
        for k in range(4):
            tokr[pl.ds(s * side + k * 320, 320), :] = tok[pl.ds(row_block(s, k), 320), :]
    wide[...] = tokr[...].T

    def put(at, value):
        act_m[at, :] = value

    hidden_part(wide, wom, wxm, ups, pl.multiple_of(place()[0] * half, 128), put, scal_m)


def second_kernel(wide, wos, wxs, ups, act_m, act, scal_o):
    c, _, _ = place()
    half = wos.shape[1]
    col = pl.multiple_of((1 - c) * half, 128)
    act[:, pl.ds(pl.multiple_of(c * half, 128), half)] = act_m[...]

    def put(at, value):
        act[at, pl.ds(col, half)] = value

    hidden_part(wide, wos, wxs, ups, col, put, scal_o)


def after_kernel(n, *refs):
    for x, out in zip(refs[:n], refs[-n:]):
        out[...] = x[...]


def after(xs, first):
    outs = tuple((x.shape, x.dtype) for x in xs)
    return call(lambda *refs: after_kernel(len(xs), *refs), "after", outs, (*xs, *first), 0, limit=16)


def call(kernel, name, outs, args, flops, scratch=(), limit=24):
    shapes = tuple(jax.ShapeDtypeStruct(shape, kind) for shape, kind in outs)
    moved = sum(x.size * x.dtype.itemsize for x in args)
    return pl.pallas_call(
        kernel,
        out_shape=shapes,
        in_specs=[VM] * len(args),
        out_specs=(VM,) * len(outs),
        scratch_shapes=scratch,
        compiler_params=pltpu.CompilerParams(vmem_limit_bytes=limit * 1024 * 1024),
        cost_estimate=pl.CostEstimate(flops=flops, bytes_accessed=moved, transcendentals=0),
        name=name,
    )(*args)


def forward_first(tok, wom, wxm, ups):
    n_feat, n_tok = tok.shape
    half = wom.shape[1]
    return call(
        first_kernel,
        "forward_first",
        (((n_tok, n_feat), BF), ((n_tok, half), BF), ((n_tok, half), BF)),
        (tok, wom, wxm, ups),
        2 * n_feat * n_tok * half,
        [pltpu.VMEM((n_feat, n_tok), BF)],
    )


def forward_second(wide, wos, wxs, ups, act_m):
    n_tok, n_feat = wide.shape
    half = wos.shape[1]
    return call(
        second_kernel,
        "forward_second",
        ((ups.shape, BF), ((n_tok, half), BF)),
        (wide, wos, wxs, ups, act_m),
        2 * n_feat * n_tok * half,
    )


def input_kernel(wom, wxm, wos, wxs, scal_m, scal_o, *refs):
    outs, whole = refs[-10:-1], refs[-1]
    dims = (((1,), (1,)), ((), ()))
    for s, wm, ws in ((0, wom, wos), (1, wxm, wxs)):
        for k in range(4):
            at = pl.ds(k * 320, 320)
            part = lax.dot_general(wm[at, :], scal_m[...], dims, preferred_element_type=F32)
            part = part + lax.dot_general(ws[at, :], scal_o[...], dims, preferred_element_type=F32)
            whole[pl.ds(row_block(s, k), 320), :] = part
    far_a, far_b, p3, p2, p1, m3, m2, m1, own = outs
    far_a[...] = whole[1280:1440, :].astype(BF)
    far_b[...] = whole[1440:1600, :].astype(BF)
    for out, k in ((p3, 3), (p2, 2), (p1, 1), (m3, 5), (m2, 6), (m1, 7)):
        out[...] = whole[k * 320 : (k + 1) * 320, :].astype(BF)
    own[...] = whole[:320, :]


def input_partial(wom, wxm, wos, wxs, scal_m, scal_o, first=()):
    n_tok = scal_m.shape[0]
    n_feat = 2 * wom.shape[0]
    return call(
        input_kernel,
        "input_partial",
        (((160, n_tok), BF),) * 2 + (((320, n_tok), BF),) * 6 + (((320, n_tok), F32),),
        (wom, wxm, wos, wxs, scal_m, scal_o, *first),
        4 * n_feat * n_tok * scal_m.shape[1],
        [pltpu.VMEM((n_feat, n_tok), F32)],
    )


def weight_kernel(s, tok, tok_s, scal, scal_s, *refs):
    for k, out in zip((2, 1, 3, 0), refs[-4:]):
        at = pl.ds(row_block(s, k), 320)
        part = jnp.dot(tok[at, :], scal[...], preferred_element_type=F32)
        part = part + jnp.dot(tok_s[at, :], scal_s[...], preferred_element_type=F32)
        out[...] = part.astype(out.dtype)


def weight_partial(s, tok, tok_s, scal, scal_s, first=()):
    n_feat, n_tok = tok.shape
    half = scal.shape[1]
    return call(
        lambda *refs: weight_kernel(s, *refs),
        "weight_partial",
        (((320, half), BF),) * 3 + (((320, half), F32),),
        (tok, tok_s, scal, scal_s, *first),
        2 * n_feat * n_tok * half,
    )


def join_kernel(parts, n_first, *refs):
    n_out = len(parts)
    ins, outs = refs[: len(refs) - n_out - n_first], refs[len(refs) - n_out :]
    at = 0
    for out, part in zip(outs, parts):
        if isinstance(part, str):
            rows = ins[at + 1].shape[0]
            add = slice(0, rows) if part == "top" else slice(rows, 2 * rows)
            keep = slice(rows, 2 * rows) if part == "top" else slice(0, rows)
            out[add, :] = (ins[at][add, :].astype(F32) + ins[at + 1][...].astype(F32)).astype(out.dtype)
            out[keep, :] = ins[at][keep, :]
            at += 2
        else:
            total = ins[at][...].astype(F32)
            for k in range(1, part):
                total = total + ins[at + k][...].astype(F32)
            out[...] = total.astype(out.dtype)
            at += part


def join(parts, operands, first=(), kinds=(BF,) * 4):
    outs, at = [], 0
    for part, kind in zip(parts, kinds):
        outs.append((operands[at].shape, kind))
        at += 2 if isinstance(part, str) else part
    return call(
        lambda *refs: join_kernel(parts, len(first), *refs), "join", tuple(outs), (*operands, *first), 0, limit=16
    )


def stack_kernel(n, *refs):
    at = 0
    for x in refs[:n]:
        refs[-1][at : at + x.shape[0], :] = x[...]
        at += x.shape[0]


def stack(parts, first=()):
    shape = (sum(x.shape[0] for x in parts), parts[0].shape[1])
    return call(lambda *refs: stack_kernel(len(parts), *refs), "stack", ((shape, BF),), (*parts, *first), 0, limit=16)[0]


def gather(tokens, up_weight):
    half = up_weight.shape[1] // 2
    own_w = lax.dynamic_slice_in_dim(up_weight, place()[0] * half, half, axis=1)
    below, above = [tokens], [tokens]

    def step():
        below.append(zup(below[-1]))
        above.append(zdown(above[-1]))

    step()
    above_o, below_o = down(own_w), up(own_w)
    cross_w = across(own_w)
    step()
    far_a, far_b = after((above_o[:160], below_o[160:]), (below[1], above[1]))
    far_o = down(far_a), up(far_b)
    (cross_w,) = after((cross_w,), (below[1], above[1]))
    above_x, below_x = down(cross_w), up(cross_w)
    step()
    far_a, far_b = after((above_x[:160], below_x[160:]), (below[2], above[2]))
    far_x = down(far_a), up(far_b)
    far_b = zup(below[3][160:])
    far_a = zdown(above[3][:160])
    tok = jnp.concatenate(above + [far_a, far_b] + below[:0:-1], axis=0)
    wom = stack([own_w, above_o, *far_o, below_o], (below[3], above[3]))
    wxm = jnp.concatenate([cross_w, above_x, *far_x, below_x], axis=0)
    return tok, wom, wxm


def shards(tokens, up_weight, upstream):
    token_rows = tokens.shape[0]
    c, _, _ = place()
    factor = 1.0 / math.sqrt(token_rows * lax.axis_size("depth") * lax.axis_size("row"))

    tok, wom, wxm = gather(tokens.T, up_weight)
    wos, wxs = sibling(wom), sibling(wxm)
    wide, act_m, scal_m = forward_first(tok, wom, wxm, upstream)
    tok_s = sibling(tok)
    activated, scal_o = forward_second(wide, wos, wxs, upstream, act_m)
    scal_s = sibling(scal_o)

    w_far, w_up, w_down, w_own = weight_partial(1, tok, tok_s, scal_m, scal_s)
    w_came = up(w_up), down(w_down), opposite(w_far)
    far_a, far_b, p3, p2, p1, m3, m2, m1, own = input_partial(wom, wxm, wos, wxs, scal_m, scal_o, (w_far,))
    z_came = zup(far_a), zdown(far_b)
    v_far, v_up, v_down, v_own = weight_partial(0, tok, tok_s, scal_m, scal_s, (far_a,))
    v_came = up(v_up), down(v_down), opposite(v_far)

    p3, m3, one = join(("top", "bottom", 4), (p3, z_came[0], m3, z_came[1], w_own, *w_came), (v_far,))
    z_came = zup(p3), zdown(m3)
    one = across(one)
    p2, m2 = join((2, 2), (p2, z_came[0], m2, z_came[1]), v_came[:2])
    z_came = zup(p2), zdown(m2)
    p1, m1, zero = join((2, 2, 5), (p1, z_came[0], m1, z_came[1], v_own, *v_came, one))
    z_came = zup(p1), zdown(m1)
    other = beside(zero)

    input_grad, total = join((3, 2), (own, *z_came, zero, other), (), (BF, F32))
    total = total * factor
    total_s = sibling(total)
    weight_grad = jnp.where(
        c == 0,
        jnp.concatenate([total, total_s], axis=1),
        jnp.concatenate([total_s, total], axis=1),
    )
    return (activated, input_grad.T, weight_grad)


def solution(mesh):
    placed = (P(("depth", "row"), "col"), P("row", "col"), P(("depth", "row"), "col"))
    return jax.shard_map(
        shards,
        mesh=mesh,
        in_specs=placed,
        out_specs=(P(("depth", "row"), "col"), P(("depth", "row"), "col"), P("row", "col")),
        check_vma=False,
    )
```

```python
import math

import jax
import jax.numpy as jnp
from jax import lax
from jax.experimental import pallas as pl
from jax.experimental.pallas import tpu as pltpu
from jax.sharding import PartitionSpec as P

AXES = ("depth", "row", "col")
BF = jnp.bfloat16
F32 = jnp.float32
VM = pl.BlockSpec(memory_space=pltpu.VMEM)


def gelu_parts(pre):
    coeff = 0.7978845608
    cube = 0.044715
    inner = coeff * (pre + cube * pre * pre * pre)
    tangent = jnp.tanh(inner)
    value = 0.5 * pre * (1.0 + tangent)
    slope = 0.5 * (1.0 + tangent) + 0.5 * pre * (1.0 - tangent * tangent) * coeff * (
        1.0 + 3.0 * cube * pre * pre
    )
    return (value, slope)


def place():
    return lax.axis_index("depth") % 2, lax.axis_index("row") // 2, lax.axis_index("row") % 2


def move(x, target):
    n_depth, n_row, n_col = (lax.axis_size(a) for a in AXES)
    pairs = []
    for d in range(n_depth):
        for r in range(n_row):
            for z in range(n_col):
                xl, c, y, xh, w = target(d // 2, d % 2, r // 2, r % 2, z)
                to = ((xl * 2 + c) * n_row + y * 2 + xh) * n_col + w
                pairs.append(((d * n_row + r) * n_col + z, to))
    return lax.ppermute(x, AXES, pairs)


def up(x):
    return move(x, lambda xl, c, y, xh, z: (xl, c, (y + 1) % 4, xh, z))


def down(x):
    return move(x, lambda xl, c, y, xh, z: (xl, c, (y + 3) % 4, xh, z))


def opposite(x):
    return move(x, lambda xl, c, y, xh, z: (xl, c, (y + 2) % 4, xh, z))


def across(x):
    return move(x, lambda xl, c, y, xh, z: (1 - xl, c, y, 1 - xh, z))


def beside(x):
    return move(x, lambda xl, c, y, xh, z: (1 - xl, c, y, xh, z))


def sibling(x):
    return move(x, lambda xl, c, y, xh, z: (xl, 1 - c, y, xh, z))


def zup(x):
    return move(x, lambda xl, c, y, xh, z: (xl, c, y, xh, (z + 1) % 8))


def zdown(x):
    return move(x, lambda xl, c, y, xh, z: (xl, c, y, xh, (z + 7) % 8))


def row_block(s, k):
    _, y, xh = place()
    other = xh if s == 0 else 1 - xh
    block = ((y + k) % 4) * 2 + other
    return pl.multiple_of(((block + 8 - lax.axis_index("col")) % 8) * 320, 64)


def hidden_part(wide, wo, wx, ups, col, put_act, put_scal):
    side, half = wo.shape
    rows = 512

    def body(i, _):
        at = pl.ds(pl.multiple_of(i * rows, rows), rows)
        pre = jnp.dot(wide[at, :side], wo[...], preferred_element_type=F32)
        pre = pre + jnp.dot(wide[at, side:], wx[...], preferred_element_type=F32)
        value, slope = gelu_parts(pre)
        put_act(at, value.astype(BF))
        put_scal[at, :] = (ups[at, pl.ds(col, half)].astype(F32) * slope).astype(BF)
        return 0

    lax.fori_loop(0, wide.shape[0] // rows, body, 0)


def first_kernel(tok, wom, wxm, ups, wide, act_m, scal_m, tokr):
    side, half = wom.shape
    for s in range(2):
        for k in range(4):
            tokr[pl.ds(s * side + k * 320, 320), :] = tok[pl.ds(row_block(s, k), 320), :]
    wide[...] = tokr[...].T

    def put(at, value):
        act_m[at, :] = value

    hidden_part(wide, wom, wxm, ups, pl.multiple_of(place()[0] * half, 128), put, scal_m)


def second_kernel(wide, wos, wxs, ups, act_m, act, scal_o):
    c, _, _ = place()
    half = wos.shape[1]
    col = pl.multiple_of((1 - c) * half, 128)
    act[:, pl.ds(pl.multiple_of(c * half, 128), half)] = act_m[...]

    def put(at, value):
        act[at, pl.ds(col, half)] = value

    hidden_part(wide, wos, wxs, ups, col, put, scal_o)


def after_kernel(n, *refs):
    for x, out in zip(refs[:n], refs[-n:]):
        out[...] = x[...]


def after(xs, first):
    outs = tuple((x.shape, x.dtype) for x in xs)
    return call(lambda *refs: after_kernel(len(xs), *refs), "after", outs, (*xs, *first), 0, limit=16)


def call(kernel, name, outs, args, flops, scratch=(), limit=24):
    shapes = tuple(jax.ShapeDtypeStruct(shape, kind) for shape, kind in outs)
    moved = sum(x.size * x.dtype.itemsize for x in args)
    return pl.pallas_call(
        kernel,
        out_shape=shapes,
        in_specs=[VM] * len(args),
        out_specs=(VM,) * len(outs),
        scratch_shapes=scratch,
        compiler_params=pltpu.CompilerParams(vmem_limit_bytes=limit * 1024 * 1024),
        cost_estimate=pl.CostEstimate(flops=flops, bytes_accessed=moved, transcendentals=0),
        name=name,
    )(*args)


def forward_first(tok, wom, wxm, ups):
    n_feat, n_tok = tok.shape
    half = wom.shape[1]
    return call(
        first_kernel,
        "forward_first",
        (((n_tok, n_feat), BF), ((n_tok, half), BF), ((n_tok, half), BF)),
        (tok, wom, wxm, ups),
        2 * n_feat * n_tok * half,
        [pltpu.VMEM((n_feat, n_tok), BF)],
    )


def forward_second(wide, wos, wxs, ups, act_m):
    n_tok, n_feat = wide.shape
    half = wos.shape[1]
    return call(
        second_kernel,
        "forward_second",
        ((ups.shape, BF), ((n_tok, half), BF)),
        (wide, wos, wxs, ups, act_m),
        2 * n_feat * n_tok * half,
    )


def input_block(wom, wxm, wos, wxs, scal_m, scal_o, k, whole):
    _, y, xh = place()
    block = (lax.axis_index("col") + k) % 8
    at = pl.ds(pl.multiple_of(((block // 2 + 4 - y) % 4) * 320, 64), 320)
    dims = (((1,), (1,)), ((), ()))

    def put(wm, ws):
        part = lax.dot_general(wm[at, :], scal_m[...], dims, preferred_element_type=F32)
        part = part + lax.dot_general(ws[at, :], scal_o[...], dims, preferred_element_type=F32)
        whole[...] = part

    pl.when(block % 2 == xh)(lambda: put(wom, wos))
    pl.when(block % 2 != xh)(lambda: put(wxm, wxs))


def input_far_kernel(wom, wxm, wos, wxs, scal_m, scal_o, far_a, far_b, whole):
    input_block(wom, wxm, wos, wxs, scal_m, scal_o, 4, whole)
    far_a[...] = whole[:160, :].astype(BF)
    far_b[...] = whole[160:, :].astype(BF)


def input_far(wom, wxm, wos, wxs, scal_m, scal_o):
    n_tok = scal_m.shape[0]
    return call(
        input_far_kernel,
        "input_far",
        (((160, n_tok), BF),) * 2,
        (wom, wxm, wos, wxs, scal_m, scal_o),
        4 * 320 * n_tok * scal_m.shape[1],
        [pltpu.VMEM((320, n_tok), F32)],
    )


def input_kernel(wom, wxm, wos, wxs, scal_m, scal_o, *refs):
    outs, whole = refs[-8:-1], refs[-1]
    dims = (((1,), (1,)), ((), ()))
    for s, wm, ws in ((0, wom, wos), (1, wxm, wxs)):
        part = lax.dot_general(wm[...], scal_m[...], dims, preferred_element_type=F32)
        part = part + lax.dot_general(ws[...], scal_o[...], dims, preferred_element_type=F32)
        for k in range(4):
            whole[pl.ds(row_block(s, k), 320), :] = part[k * 320 : (k + 1) * 320, :]
    for out, k in zip(outs, (3, 2, 1, 5, 6, 7, 0)):
        out[...] = whole[k * 320 : (k + 1) * 320, :].astype(out.dtype)


def input_rest(wom, wxm, wos, wxs, scal_m, scal_o, first):
    n_tok = scal_m.shape[0]
    n_feat = 2 * wom.shape[0]
    return call(
        input_kernel,
        "input_rest",
        (((320, n_tok), BF),) * 6 + (((320, n_tok), F32),),
        (wom, wxm, wos, wxs, scal_m, scal_o, *first),
        4 * n_feat * n_tok * scal_m.shape[1],
        [pltpu.VMEM((n_feat, n_tok), F32)],
    )


def weight_kernel(s, tok, tok_s, scal, scal_s, *refs):
    for k, out in zip((2, 1, 3, 0), refs[-4:]):
        at = pl.ds(row_block(s, k), 320)
        part = jnp.dot(tok[at, :], scal[...], preferred_element_type=F32)
        part = part + jnp.dot(tok_s[at, :], scal_s[...], preferred_element_type=F32)
        out[...] = part.astype(out.dtype)


def weight_partial(s, tok, tok_s, scal, scal_s, first=()):
    n_feat, n_tok = tok.shape
    half = scal.shape[1]
    return call(
        lambda *refs: weight_kernel(s, *refs),
        "weight_partial",
        (((320, half), BF),) * 3 + (((320, half), F32),),
        (tok, tok_s, scal, scal_s, *first),
        2 * n_feat * n_tok * half,
    )


def join_kernel(parts, n_first, *refs):
    n_out = len(parts)
    ins, outs = refs[: len(refs) - n_out - n_first], refs[len(refs) - n_out :]
    at = 0
    for out, part in zip(outs, parts):
        if isinstance(part, str):
            rows = ins[at + 1].shape[0]
            add = slice(0, rows) if part == "top" else slice(rows, 2 * rows)
            keep = slice(rows, 2 * rows) if part == "top" else slice(0, rows)
            out[add, :] = (ins[at][add, :].astype(F32) + ins[at + 1][...].astype(F32)).astype(out.dtype)
            out[keep, :] = ins[at][keep, :]
            at += 2
        else:
            total = ins[at][...].astype(F32)
            for k in range(1, part):
                total = total + ins[at + k][...].astype(F32)
            out[...] = total.astype(out.dtype)
            at += part


def join(parts, operands, first=(), kinds=(BF,) * 4):
    outs, at = [], 0
    for part, kind in zip(parts, kinds):
        outs.append((operands[at].shape, kind))
        at += 2 if isinstance(part, str) else part
    return call(
        lambda *refs: join_kernel(parts, len(first), *refs), "join", tuple(outs), (*operands, *first), 0, limit=16
    )


def stack_kernel(n, *refs):
    at = 0
    for x in refs[:n]:
        refs[-1][at : at + x.shape[0], :] = x[...]
        at += x.shape[0]


def stack(parts, first=()):
    shape = (sum(x.shape[0] for x in parts), parts[0].shape[1])
    return call(lambda *refs: stack_kernel(len(parts), *refs), "stack", ((shape, BF),), (*parts, *first), 0, limit=16)[0]


def gather(tokens, up_weight):
    half = up_weight.shape[1] // 2
    own_w = lax.dynamic_slice_in_dim(up_weight, place()[0] * half, half, axis=1)
    below, above = [tokens], [tokens]

    def step():
        below.append(zup(below[-1]))
        above.append(zdown(above[-1]))

    step()
    above_o, below_o = down(own_w), up(own_w)
    cross_w = across(own_w)
    step()
    far_a, far_b = after((above_o[:160], below_o[160:]), (below[1], above[1]))
    far_o = down(far_a), up(far_b)
    (cross_w,) = after((cross_w,), (below[1], above[1]))
    above_x, below_x = down(cross_w), up(cross_w)
    step()
    far_a, far_b = after((above_x[:160], below_x[160:]), (below[2], above[2]))
    far_x = down(far_a), up(far_b)
    far_b = zup(below[3][160:])
    far_a = zdown(above[3][:160])
    tok = jnp.concatenate(above + [far_a, far_b] + below[:0:-1], axis=0)
    wom = stack([own_w, above_o, *far_o, below_o], (below[3], above[3]))
    wxm = jnp.concatenate([cross_w, above_x, *far_x, below_x], axis=0)
    return tok, wom, wxm


def shards(tokens, up_weight, upstream):
    token_rows = tokens.shape[0]
    c, _, _ = place()
    factor = 1.0 / math.sqrt(token_rows * lax.axis_size("depth") * lax.axis_size("row"))

    tok, wom, wxm = gather(tokens.T, up_weight)
    wos, wxs = sibling(wom), sibling(wxm)
    wide, act_m, scal_m = forward_first(tok, wom, wxm, upstream)
    tok_s = sibling(tok)
    activated, scal_o = forward_second(wide, wos, wxs, upstream, act_m)
    scal_s = sibling(scal_o)

    parts = (wom, wxm, wos, wxs, scal_m, scal_o)
    far_a, far_b = input_far(*parts)
    w_far, w_up, w_down, w_own = weight_partial(1, tok, tok_s, scal_m, scal_s, (far_a,))
    w_came = up(w_up), down(w_down), opposite(w_far)
    far_a, far_b = after((far_a, far_b), (w_far,))
    z_came = zup(far_a), zdown(far_b)
    p3, p2, p1, m3, m2, m1, own = input_rest(*parts, (w_far,))
    v_far, v_up, v_down, v_own = weight_partial(0, tok, tok_s, scal_m, scal_s, (p3,))
    v_came = up(v_up), down(v_down), opposite(v_far)

    p3, m3 = join(("top", "bottom"), (p3, z_came[0], m3, z_came[1]), (v_far,))
    z_came = zup(p3), zdown(m3)
    (one,) = join((4,), (w_own, *w_came), (p3,))
    cross = across(one)
    p2, m2 = join((2, 2), (p2, z_came[0], m2, z_came[1]), (one, v_came[2]))
    z_came = zup(p2), zdown(m2)
    p1, m1, zero = join((2, 2, 5), (p1, z_came[0], m1, z_came[1], v_own, *v_came, cross))
    z_came = zup(p1), zdown(m1)
    other = beside(zero)

    input_grad, total = join((3, 2), (own, *z_came, zero, other), (), (BF, F32))
    total = total * factor
    total_s = sibling(total)
    weight_grad = jnp.where(
        c == 0,
        jnp.concatenate([total, total_s], axis=1),
        jnp.concatenate([total_s, total], axis=1),
    )
    return (activated, input_grad.T, weight_grad)


def solution(mesh):
    placed = (P(("depth", "row"), "col"), P("row", "col"), P(("depth", "row"), "col"))
    return jax.shard_map(
        shards,
        mesh=mesh,
        in_specs=placed,
        out_specs=(P(("depth", "row"), "col"), P(("depth", "row"), "col"), P("row", "col")),
        check_vma=False,
    )
```

```python
import math

import jax
import jax.numpy as jnp
from jax import lax
from jax.experimental import pallas as pl
from jax.experimental.pallas import tpu as pltpu
from jax.sharding import PartitionSpec as P

AXES = ("depth", "row", "col")
BF = jnp.bfloat16
F32 = jnp.float32
VM = pl.BlockSpec(memory_space=pltpu.VMEM)


def gelu_parts(pre):
    coeff = 0.7978845608
    cube = 0.044715
    inner = coeff * (pre + cube * pre * pre * pre)
    tangent = jnp.tanh(inner)
    value = 0.5 * pre * (1.0 + tangent)
    slope = 0.5 * (1.0 + tangent) + 0.5 * pre * (1.0 - tangent * tangent) * coeff * (
        1.0 + 3.0 * cube * pre * pre
    )
    return (value, slope)


def place():
    return lax.axis_index("depth") % 2, lax.axis_index("row") // 2, lax.axis_index("row") % 2


def move(x, target):
    n_depth, n_row, n_col = (lax.axis_size(a) for a in AXES)
    pairs = []
    for d in range(n_depth):
        for r in range(n_row):
            for z in range(n_col):
                xl, c, y, xh, w = target(d // 2, d % 2, r // 2, r % 2, z)
                to = ((xl * 2 + c) * n_row + y * 2 + xh) * n_col + w
                pairs.append(((d * n_row + r) * n_col + z, to))
    return lax.ppermute(x, AXES, pairs)


def up(x):
    return move(x, lambda xl, c, y, xh, z: (xl, c, (y + 1) % 4, xh, z))


def down(x):
    return move(x, lambda xl, c, y, xh, z: (xl, c, (y + 3) % 4, xh, z))


def opposite(x):
    return move(x, lambda xl, c, y, xh, z: (xl, c, (y + 2) % 4, xh, z))


def across(x):
    return move(x, lambda xl, c, y, xh, z: (1 - xl, c, y, 1 - xh, z))


def beside(x):
    return move(x, lambda xl, c, y, xh, z: (1 - xl, c, y, xh, z))


def sibling(x):
    return move(x, lambda xl, c, y, xh, z: (xl, 1 - c, y, xh, z))


def zup(x):
    return move(x, lambda xl, c, y, xh, z: (xl, c, y, xh, (z + 1) % 8))


def zdown(x):
    return move(x, lambda xl, c, y, xh, z: (xl, c, y, xh, (z + 7) % 8))


def row_block(s, k):
    _, y, xh = place()
    other = xh if s == 0 else 1 - xh
    block = ((y + k) % 4) * 2 + other
    return pl.multiple_of(((block + 8 - lax.axis_index("col")) % 8) * 320, 64)


def hidden_part(wide, wo, wx, ups, col, put_act, put_scal):
    side, half = wo.shape
    rows = 512

    def body(i, _):
        at = pl.ds(pl.multiple_of(i * rows, rows), rows)
        pre = jnp.dot(wide[at, :side], wo[...], preferred_element_type=F32)
        pre = pre + jnp.dot(wide[at, side:], wx[...], preferred_element_type=F32)
        value, slope = gelu_parts(pre)
        put_act(at, value.astype(BF))
        put_scal[at, :] = (ups[at, pl.ds(col, half)].astype(F32) * slope).astype(BF)
        return 0

    lax.fori_loop(0, wide.shape[0] // rows, body, 0)


def first_kernel(tok, wom, wxm, ups, wide, act_m, scal_m, tokr):
    side, half = wom.shape
    for s in range(2):
        for k in range(4):
            tokr[pl.ds(s * side + k * 320, 320), :] = tok[pl.ds(row_block(s, k), 320), :]
    wide[...] = tokr[...].T

    def put(at, value):
        act_m[at, :] = value

    hidden_part(wide, wom, wxm, ups, pl.multiple_of(place()[0] * half, 128), put, scal_m)


def second_kernel(wide, wos, wxs, ups, act_m, act, scal_o):
    c, _, _ = place()
    half = wos.shape[1]
    col = pl.multiple_of((1 - c) * half, 128)
    act[:, pl.ds(pl.multiple_of(c * half, 128), half)] = act_m[...]

    def put(at, value):
        act[at, pl.ds(col, half)] = value

    hidden_part(wide, wos, wxs, ups, col, put, scal_o)


def after_kernel(n, *refs):
    for x, out in zip(refs[:n], refs[-n:]):
        out[...] = x[...]


def after(xs, first):
    outs = tuple((x.shape, x.dtype) for x in xs)
    return call(lambda *refs: after_kernel(len(xs), *refs), "after", outs, (*xs, *first), 0, limit=16)


def call(kernel, name, outs, args, flops, scratch=(), limit=24):
    shapes = tuple(jax.ShapeDtypeStruct(shape, kind) for shape, kind in outs)
    moved = sum(x.size * x.dtype.itemsize for x in args)
    return pl.pallas_call(
        kernel,
        out_shape=shapes,
        in_specs=[VM] * len(args),
        out_specs=(VM,) * len(outs),
        scratch_shapes=scratch,
        compiler_params=pltpu.CompilerParams(vmem_limit_bytes=limit * 1024 * 1024),
        cost_estimate=pl.CostEstimate(flops=flops, bytes_accessed=moved, transcendentals=0),
        name=name,
    )(*args)


def forward_first(tok, wom, wxm, ups):
    n_feat, n_tok = tok.shape
    half = wom.shape[1]
    return call(
        first_kernel,
        "forward_first",
        (((n_tok, n_feat), BF), ((n_tok, half), BF), ((n_tok, half), BF)),
        (tok, wom, wxm, ups),
        2 * n_feat * n_tok * half,
        [pltpu.VMEM((n_feat, n_tok), BF)],
    )


def forward_second(wide, wos, wxs, ups, act_m):
    n_tok, n_feat = wide.shape
    half = wos.shape[1]
    return call(
        second_kernel,
        "forward_second",
        ((ups.shape, BF), ((n_tok, half), BF)),
        (wide, wos, wxs, ups, act_m),
        2 * n_feat * n_tok * half,
    )


def input_block(wom, wxm, wos, wxs, scal_m, scal_o, k, whole):
    _, y, xh = place()
    block = (lax.axis_index("col") + k) % 8
    at = pl.ds(pl.multiple_of(((block // 2 + 4 - y) % 4) * 320, 64), 320)
    dims = (((1,), (1,)), ((), ()))

    def put(wm, ws):
        part = lax.dot_general(wm[at, :], scal_m[...], dims, preferred_element_type=F32)
        part = part + lax.dot_general(ws[at, :], scal_o[...], dims, preferred_element_type=F32)
        whole[...] = part

    pl.when(block % 2 == xh)(lambda: put(wom, wos))
    pl.when(block % 2 != xh)(lambda: put(wxm, wxs))


def input_far_kernel(wom, wxm, wos, wxs, scal_m, scal_o, far_a, far_b, whole):
    input_block(wom, wxm, wos, wxs, scal_m, scal_o, 4, whole)
    far_a[...] = whole[:160, :].astype(BF)
    far_b[...] = whole[160:, :].astype(BF)


def input_far(wom, wxm, wos, wxs, scal_m, scal_o):
    n_tok = scal_m.shape[0]
    return call(
        input_far_kernel,
        "input_far",
        (((160, n_tok), BF),) * 2,
        (wom, wxm, wos, wxs, scal_m, scal_o),
        4 * 320 * n_tok * scal_m.shape[1],
        [pltpu.VMEM((320, n_tok), F32)],
    )


def input_kernel(wom, wxm, wos, wxs, scal_m, scal_o, *refs):
    outs, whole = refs[-8:-1], refs[-1]
    dims = (((1,), (1,)), ((), ()))
    for s, wm, ws in ((0, wom, wos), (1, wxm, wxs)):
        part = lax.dot_general(wm[...], scal_m[...], dims, preferred_element_type=F32)
        part = part + lax.dot_general(ws[...], scal_o[...], dims, preferred_element_type=F32)
        for k in range(4):
            whole[pl.ds(row_block(s, k), 320), :] = part[k * 320 : (k + 1) * 320, :]
    for out, k in zip(outs, (3, 2, 1, 5, 6, 7, 0)):
        out[...] = whole[k * 320 : (k + 1) * 320, :].astype(out.dtype)


def input_rest(wom, wxm, wos, wxs, scal_m, scal_o, first):
    n_tok = scal_m.shape[0]
    n_feat = 2 * wom.shape[0]
    return call(
        input_kernel,
        "input_rest",
        (((320, n_tok), BF),) * 6 + (((320, n_tok), F32),),
        (wom, wxm, wos, wxs, scal_m, scal_o, *first),
        4 * n_feat * n_tok * scal_m.shape[1],
        [pltpu.VMEM((n_feat, n_tok), F32)],
    )


def weight_kernel(s, tok, tok_s, scal, scal_s, *refs):
    for k, out in zip((2, 1, 3, 0), refs[-4:]):
        at = pl.ds(row_block(s, k), 320)
        part = jnp.dot(tok[at, :], scal[...], preferred_element_type=F32)
        part = part + jnp.dot(tok_s[at, :], scal_s[...], preferred_element_type=F32)
        out[...] = part.astype(out.dtype)


def weight_partial(s, tok, tok_s, scal, scal_s, first=()):
    n_feat, n_tok = tok.shape
    half = scal.shape[1]
    return call(
        lambda *refs: weight_kernel(s, *refs),
        "weight_partial",
        (((320, half), BF),) * 3 + (((320, half), F32),),
        (tok, tok_s, scal, scal_s, *first),
        2 * n_feat * n_tok * half,
    )


def join_kernel(parts, n_first, *refs):
    n_out = len(parts)
    ins, outs = refs[: len(refs) - n_out - n_first], refs[len(refs) - n_out :]
    at = 0
    for out, part in zip(outs, parts):
        if isinstance(part, str):
            rows = ins[at + 1].shape[0]
            add = slice(0, rows) if part == "top" else slice(rows, 2 * rows)
            keep = slice(rows, 2 * rows) if part == "top" else slice(0, rows)
            out[add, :] = (ins[at][add, :].astype(F32) + ins[at + 1][...].astype(F32)).astype(out.dtype)
            out[keep, :] = ins[at][keep, :]
            at += 2
        else:
            total = ins[at][...].astype(F32)
            for k in range(1, part):
                total = total + ins[at + k][...].astype(F32)
            out[...] = total.astype(out.dtype)
            at += part


def join(parts, operands, first=(), kinds=(BF,) * 4):
    outs, at = [], 0
    for part, kind in zip(parts, kinds):
        outs.append((operands[at].shape, kind))
        at += 2 if isinstance(part, str) else part
    return call(
        lambda *refs: join_kernel(parts, len(first), *refs), "join", tuple(outs), (*operands, *first), 0, limit=16
    )


def finish_kernel(factor, zero, other, zero_s, other_s, out):
    c, _, _ = place()
    half = zero.shape[1]
    for left, right, col in ((zero, other, c * half), (zero_s, other_s, (1 - c) * half)):
        total = left[...].astype(F32) + right[...].astype(F32)
        out[:, pl.ds(pl.multiple_of(col, 128), half)] = total * factor


def finish(factor, zero, other, zero_s, other_s):
    shape = (zero.shape[0], 2 * zero.shape[1])
    args = (zero, other, zero_s, other_s)
    return call(lambda *refs: finish_kernel(factor, *refs), "finish", ((shape, F32),), args, 0, limit=16)[0]


def stack_kernel(n, *refs):
    at = 0
    for x in refs[:n]:
        refs[-1][at : at + x.shape[0], :] = x[...]
        at += x.shape[0]


def stack(parts, first=()):
    shape = (sum(x.shape[0] for x in parts), parts[0].shape[1])
    return call(lambda *refs: stack_kernel(len(parts), *refs), "stack", ((shape, BF),), (*parts, *first), 0, limit=16)[0]


def gather(tokens, up_weight):
    half = up_weight.shape[1] // 2
    own_w = lax.dynamic_slice_in_dim(up_weight, place()[0] * half, half, axis=1)
    below, above = [tokens], [tokens]

    def step():
        below.append(zup(below[-1]))
        above.append(zdown(above[-1]))

    step()
    above_o, below_o = down(own_w), up(own_w)
    cross_w = across(own_w)
    step()
    far_a, far_b = after((above_o[:160], below_o[160:]), (below[1], above[1]))
    far_o = down(far_a), up(far_b)
    (cross_w,) = after((cross_w,), (below[1], above[1]))
    above_x, below_x = down(cross_w), up(cross_w)
    step()
    far_a, far_b = after((above_x[:160], below_x[160:]), (below[2], above[2]))
    far_x = down(far_a), up(far_b)
    far_b = zup(below[3][160:])
    far_a = zdown(above[3][:160])
    tok = jnp.concatenate(above + [far_a, far_b] + below[:0:-1], axis=0)
    wom = stack([own_w, above_o, *far_o, below_o], (below[3], above[3]))
    wxm = jnp.concatenate([cross_w, above_x, *far_x, below_x], axis=0)
    return tok, wom, wxm


def shards(tokens, up_weight, upstream):
    token_rows = tokens.shape[0]
    factor = 1.0 / math.sqrt(token_rows * lax.axis_size("depth") * lax.axis_size("row"))

    tok, wom, wxm = gather(tokens.T, up_weight)
    wos, wxs = sibling(wom), sibling(wxm)
    wide, act_m, scal_m = forward_first(tok, wom, wxm, upstream)
    tok_s = sibling(tok)
    activated, scal_o = forward_second(wide, wos, wxs, upstream, act_m)
    scal_s = sibling(scal_o)

    parts = (wom, wxm, wos, wxs, scal_m, scal_o)
    far_a, far_b = input_far(*parts)
    w_far, w_up, w_down, w_own = weight_partial(1, tok, tok_s, scal_m, scal_s, (far_a,))
    w_came = up(w_up), down(w_down), opposite(w_far)
    far_a, far_b = after((far_a, far_b), (w_far,))
    z_came = zup(far_a), zdown(far_b)
    p3, p2, p1, m3, m2, m1, own = input_rest(*parts, (w_far,))
    v_far, v_up, v_down, v_own = weight_partial(0, tok, tok_s, scal_m, scal_s, (p3,))
    v_came = up(v_up), down(v_down), opposite(v_far)

    p3, m3 = join(("top", "bottom"), (p3, z_came[0], m3, z_came[1]), (v_far,))
    z_came = zup(p3), zdown(m3)
    (one,) = join((4,), (w_own, *w_came), (p3,))
    cross = across(one)
    p2, m2 = join((2, 2), (p2, z_came[0], m2, z_came[1]), (one, v_came[2]))
    z_came = zup(p2), zdown(m2)
    p1, m1, zero = join((2, 2, 5), (p1, z_came[0], m1, z_came[1], v_own, *v_came, cross))
    z_came = zup(p1), zdown(m1)
    other = beside(zero)

    zero_s = sibling(zero)
    (other,) = after((other,), z_came)
    other_s = sibling(other)
    (input_grad,) = join((3,), (own, *z_came))
    weight_grad = finish(factor, zero, other, zero_s, other_s)
    return (activated, input_grad.T, weight_grad)


def solution(mesh):
    placed = (P(("depth", "row"), "col"), P("row", "col"), P(("depth", "row"), "col"))
    return jax.shard_map(
        shards,
        mesh=mesh,
        in_specs=placed,
        out_specs=(P(("depth", "row"), "col"), P(("depth", "row"), "col"), P("row", "col")),
        check_vma=False,
    )
```

```python
import math

import jax
import jax.numpy as jnp
from jax import lax
from jax.experimental import pallas as pl
from jax.experimental.pallas import tpu as pltpu
from jax.sharding import PartitionSpec as P

AXES = ("depth", "row", "col")
BF = jnp.bfloat16
F32 = jnp.float32
VM = pl.BlockSpec(memory_space=pltpu.VMEM)


def gelu_parts(pre):
    coeff = 0.7978845608
    cube = 0.044715
    inner = coeff * (pre + cube * pre * pre * pre)
    tangent = jnp.tanh(inner)
    value = 0.5 * pre * (1.0 + tangent)
    slope = 0.5 * (1.0 + tangent) + 0.5 * pre * (1.0 - tangent * tangent) * coeff * (
        1.0 + 3.0 * cube * pre * pre
    )
    return (value, slope)


def place():
    return lax.axis_index("depth") % 2, lax.axis_index("row") // 2, lax.axis_index("row") % 2


def move(x, target):
    n_depth, n_row, n_col = (lax.axis_size(a) for a in AXES)
    pairs = []
    for d in range(n_depth):
        for r in range(n_row):
            for z in range(n_col):
                xl, c, y, xh, w = target(d // 2, d % 2, r // 2, r % 2, z)
                to = ((xl * 2 + c) * n_row + y * 2 + xh) * n_col + w
                pairs.append(((d * n_row + r) * n_col + z, to))
    return lax.ppermute(x, AXES, pairs)


def up(x):
    return move(x, lambda xl, c, y, xh, z: (xl, c, (y + 1) % 4, xh, z))


def down(x):
    return move(x, lambda xl, c, y, xh, z: (xl, c, (y + 3) % 4, xh, z))


def opposite(x):
    return move(x, lambda xl, c, y, xh, z: (xl, c, (y + 2) % 4, xh, z))


def across(x):
    return move(x, lambda xl, c, y, xh, z: (1 - xl, c, y, 1 - xh, z))


def beside(x):
    return move(x, lambda xl, c, y, xh, z: (1 - xl, c, y, xh, z))


def sibling(x):
    return move(x, lambda xl, c, y, xh, z: (xl, 1 - c, y, xh, z))


def zup(x):
    return move(x, lambda xl, c, y, xh, z: (xl, c, y, xh, (z + 1) % 8))


def zdown(x):
    return move(x, lambda xl, c, y, xh, z: (xl, c, y, xh, (z + 7) % 8))


def row_block(s, k):
    _, y, xh = place()
    other = xh if s == 0 else 1 - xh
    block = ((y + k) % 4) * 2 + other
    return pl.multiple_of(((block + 8 - lax.axis_index("col")) % 8) * 320, 64)


def hidden_part(wide, wo, wx, ups, col, put_act, put_scal):
    side, half = wo.shape
    rows = 512

    def body(i, _):
        at = pl.ds(pl.multiple_of(i * rows, rows), rows)
        pre = jnp.dot(wide[at, :side], wo[...], preferred_element_type=F32)
        pre = pre + jnp.dot(wide[at, side:], wx[...], preferred_element_type=F32)
        value, slope = gelu_parts(pre)
        put_act(at, value.astype(BF))
        put_scal[at, :] = (ups[at, pl.ds(col, half)].astype(F32) * slope).astype(BF)
        return 0

    lax.fori_loop(0, wide.shape[0] // rows, body, 0)


def first_kernel(tok, wom, wxm, ups, wide, act_m, scal_m, tokr):
    side, half = wom.shape
    for s in range(2):
        for k in range(4):
            tokr[pl.ds(s * side + k * 320, 320), :] = tok[pl.ds(row_block(s, k), 320), :]
    wide[...] = tokr[...].T

    def put(at, value):
        act_m[at, :] = value

    hidden_part(wide, wom, wxm, ups, pl.multiple_of(place()[0] * half, 128), put, scal_m)


def middle_kernel(wide, wos, part):
    part[...] = jnp.dot(wide[:, : wos.shape[0]], wos[...], preferred_element_type=F32)


def second_kernel(wide, part, wxs, ups, act_m, act, scal_o):
    c, _, _ = place()
    side, half = wxs.shape
    cols = pl.ds(pl.multiple_of((1 - c) * half, 128), half)
    act[:, pl.ds(pl.multiple_of(c * half, 128), half)] = act_m[...]
    pre = part[...] + jnp.dot(wide[:, side:], wxs[...], preferred_element_type=F32)
    value, slope = gelu_parts(pre)
    act[:, cols] = value.astype(BF)
    scal_o[...] = (ups[:, cols].astype(F32) * slope).astype(BF)


def after_kernel(n, *refs):
    for x, out in zip(refs[:n], refs[-n:]):
        out[...] = x[...]


def after(xs, first):
    outs = tuple((x.shape, x.dtype) for x in xs)
    return call(lambda *refs: after_kernel(len(xs), *refs), "after", outs, (*xs, *first), 0, limit=16)


def call(kernel, name, outs, args, flops, scratch=(), limit=24):
    shapes = tuple(jax.ShapeDtypeStruct(shape, kind) for shape, kind in outs)
    moved = sum(x.size * x.dtype.itemsize for x in args)
    return pl.pallas_call(
        kernel,
        out_shape=shapes,
        in_specs=[VM] * len(args),
        out_specs=(VM,) * len(outs),
        scratch_shapes=scratch,
        compiler_params=pltpu.CompilerParams(vmem_limit_bytes=limit * 1024 * 1024),
        cost_estimate=pl.CostEstimate(flops=flops, bytes_accessed=moved, transcendentals=0),
        name=name,
    )(*args)


def forward_first(tok, wom, wxm, ups):
    n_feat, n_tok = tok.shape
    half = wom.shape[1]
    return call(
        first_kernel,
        "forward_first",
        (((n_tok, n_feat), BF), ((n_tok, half), BF), ((n_tok, half), BF)),
        (tok, wom, wxm, ups),
        2 * n_feat * n_tok * half,
        [pltpu.VMEM((n_feat, n_tok), BF)],
    )


def forward_second(wide, wos, wxs, ups, act_m):
    n_tok, n_feat = wide.shape
    half = wos.shape[1]
    flops = n_feat * n_tok * half
    (part,) = call(middle_kernel, "forward_middle", (((n_tok, half), F32),), (wide, wos), flops)
    return call(
        second_kernel,
        "forward_second",
        ((ups.shape, BF), ((n_tok, half), BF)),
        (wide, part, wxs, ups, act_m),
        flops,
    )


def input_block(wom, wxm, wos, wxs, scal_m, scal_o, k, whole):
    _, y, xh = place()
    block = (lax.axis_index("col") + k) % 8
    at = pl.ds(pl.multiple_of(((block // 2 + 4 - y) % 4) * 320, 64), 320)
    dims = (((1,), (1,)), ((), ()))

    def put(wm, ws):
        part = lax.dot_general(wm[at, :], scal_m[...], dims, preferred_element_type=F32)
        part = part + lax.dot_general(ws[at, :], scal_o[...], dims, preferred_element_type=F32)
        whole[...] = part

    pl.when(block % 2 == xh)(lambda: put(wom, wos))
    pl.when(block % 2 != xh)(lambda: put(wxm, wxs))


def input_far_kernel(wom, wxm, wos, wxs, scal_m, scal_o, far_a, far_b, whole):
    input_block(wom, wxm, wos, wxs, scal_m, scal_o, 4, whole)
    far_a[...] = whole[:160, :].astype(BF)
    far_b[...] = whole[160:, :].astype(BF)


def input_far(wom, wxm, wos, wxs, scal_m, scal_o):
    n_tok = scal_m.shape[0]
    return call(
        input_far_kernel,
        "input_far",
        (((160, n_tok), BF),) * 2,
        (wom, wxm, wos, wxs, scal_m, scal_o),
        4 * 320 * n_tok * scal_m.shape[1],
        [pltpu.VMEM((320, n_tok), F32)],
    )


def input_kernel(wom, wxm, wos, wxs, scal_m, scal_o, *refs):
    outs, whole = refs[-8:-1], refs[-1]
    dims = (((1,), (1,)), ((), ()))
    for s, wm, ws in ((0, wom, wos), (1, wxm, wxs)):
        part = lax.dot_general(wm[...], scal_m[...], dims, preferred_element_type=F32)
        part = part + lax.dot_general(ws[...], scal_o[...], dims, preferred_element_type=F32)
        for k in range(4):
            whole[pl.ds(row_block(s, k), 320), :] = part[k * 320 : (k + 1) * 320, :]
    for out, k in zip(outs, (3, 2, 1, 5, 6, 7, 0)):
        out[...] = whole[k * 320 : (k + 1) * 320, :].astype(out.dtype)


def input_rest(wom, wxm, wos, wxs, scal_m, scal_o, first):
    n_tok = scal_m.shape[0]
    n_feat = 2 * wom.shape[0]
    return call(
        input_kernel,
        "input_rest",
        (((320, n_tok), BF),) * 6 + (((320, n_tok), F32),),
        (wom, wxm, wos, wxs, scal_m, scal_o, *first),
        4 * n_feat * n_tok * scal_m.shape[1],
        [pltpu.VMEM((n_feat, n_tok), F32)],
    )


def weight_kernel(s, tok, tok_s, scal, scal_s, *refs):
    for k, out in zip((2, 1, 3, 0), refs[-4:]):
        at = pl.ds(row_block(s, k), 320)
        part = jnp.dot(tok[at, :], scal[...], preferred_element_type=F32)
        part = part + jnp.dot(tok_s[at, :], scal_s[...], preferred_element_type=F32)
        out[...] = part.astype(out.dtype)


def weight_partial(s, tok, tok_s, scal, scal_s, first=()):
    n_feat, n_tok = tok.shape
    half = scal.shape[1]
    return call(
        lambda *refs: weight_kernel(s, *refs),
        "weight_partial",
        (((320, half), BF),) * 3 + (((320, half), F32),),
        (tok, tok_s, scal, scal_s, *first),
        2 * n_feat * n_tok * half,
    )


def join_kernel(parts, n_first, *refs):
    n_out = len(parts)
    ins, outs = refs[: len(refs) - n_out - n_first], refs[len(refs) - n_out :]
    at = 0
    for out, part in zip(outs, parts):
        if isinstance(part, str):
            rows = ins[at + 1].shape[0]
            add = slice(0, rows) if part == "top" else slice(rows, 2 * rows)
            keep = slice(rows, 2 * rows) if part == "top" else slice(0, rows)
            out[add, :] = (ins[at][add, :].astype(F32) + ins[at + 1][...].astype(F32)).astype(out.dtype)
            out[keep, :] = ins[at][keep, :]
            at += 2
        else:
            total = ins[at][...].astype(F32)
            for k in range(1, part):
                total = total + ins[at + k][...].astype(F32)
            out[...] = total.astype(out.dtype)
            at += part


def join(parts, operands, first=(), kinds=(BF,) * 4):
    outs, at = [], 0
    for part, kind in zip(parts, kinds):
        outs.append((operands[at].shape, kind))
        at += 2 if isinstance(part, str) else part
    return call(
        lambda *refs: join_kernel(parts, len(first), *refs), "join", tuple(outs), (*operands, *first), 0, limit=16
    )


def finish_kernel(factor, zero, other, zero_s, other_s, out):
    c, _, _ = place()
    half = zero.shape[1]
    for left, right, col in ((zero, other, c * half), (zero_s, other_s, (1 - c) * half)):
        total = left[...].astype(F32) + right[...].astype(F32)
        out[:, pl.ds(pl.multiple_of(col, 128), half)] = total * factor


def finish(factor, zero, other, zero_s, other_s):
    shape = (zero.shape[0], 2 * zero.shape[1])
    args = (zero, other, zero_s, other_s)
    return call(lambda *refs: finish_kernel(factor, *refs), "finish", ((shape, F32),), args, 0, limit=16)[0]


def stack_kernel(n, *refs):
    at = 0
    for x in refs[:n]:
        refs[-1][at : at + x.shape[0], :] = x[...]
        at += x.shape[0]


def stack(parts, first=()):
    shape = (sum(x.shape[0] for x in parts), parts[0].shape[1])
    return call(lambda *refs: stack_kernel(len(parts), *refs), "stack", ((shape, BF),), (*parts, *first), 0, limit=16)[0]


def gather(tokens, up_weight):
    half = up_weight.shape[1] // 2
    own_w = lax.dynamic_slice_in_dim(up_weight, place()[0] * half, half, axis=1)
    below, above = [tokens], [tokens]

    def step():
        below.append(zup(below[-1]))
        above.append(zdown(above[-1]))

    step()
    above_o, below_o = down(own_w), up(own_w)
    cross_w = across(own_w)
    step()
    far_a, far_b = after((above_o[:160], below_o[160:]), (below[1], above[1]))
    far_o = down(far_a), up(far_b)
    (cross_w,) = after((cross_w,), (below[1], above[1]))
    above_x, below_x = down(cross_w), up(cross_w)
    step()
    far_a, far_b = after((above_x[:160], below_x[160:]), (below[2], above[2]))
    far_x = down(far_a), up(far_b)
    far_b = zup(below[3][160:])
    far_a = zdown(above[3][:160])
    tok = jnp.concatenate(above + [far_a, far_b] + below[:0:-1], axis=0)
    wom = stack([own_w, above_o, *far_o, below_o], (below[3], above[3]))
    wxm = jnp.concatenate([cross_w, above_x, *far_x, below_x], axis=0)
    return tok, wom, wxm


def shards(tokens, up_weight, upstream):
    token_rows = tokens.shape[0]
    factor = 1.0 / math.sqrt(token_rows * lax.axis_size("depth") * lax.axis_size("row"))

    tok, wom, wxm = gather(tokens.T, up_weight)
    wos, wxs = sibling(wom), sibling(wxm)
    wide, act_m, scal_m = forward_first(tok, wom, wxm, upstream)
    tok_s = sibling(tok)
    activated, scal_o = forward_second(wide, wos, wxs, upstream, act_m)
    scal_s = sibling(scal_o)

    parts = (wom, wxm, wos, wxs, scal_m, scal_o)
    far_a, far_b = input_far(*parts)
    w_far, w_up, w_down, w_own = weight_partial(1, tok, tok_s, scal_m, scal_s, (far_a,))
    w_came = up(w_up), down(w_down), opposite(w_far)
    far_a, far_b = after((far_a, far_b), (w_far,))
    z_came = zup(far_a), zdown(far_b)
    p3, p2, p1, m3, m2, m1, own = input_rest(*parts, (w_far,))
    v_far, v_up, v_down, v_own = weight_partial(0, tok, tok_s, scal_m, scal_s, (p3,))
    v_came = up(v_up), down(v_down), opposite(v_far)

    p3, m3 = join(("top", "bottom"), (p3, z_came[0], m3, z_came[1]), (v_far,))
    z_came = zup(p3), zdown(m3)
    (one,) = join((4,), (w_own, *w_came), (p3,))
    cross = across(one)
    p2, m2 = join((2, 2), (p2, z_came[0], m2, z_came[1]), (one, v_came[2]))
    z_came = zup(p2), zdown(m2)
    p1, m1, zero = join((2, 2, 5), (p1, z_came[0], m1, z_came[1], v_own, *v_came, cross))
    z_came = zup(p1), zdown(m1)
    other = beside(zero)

    zero_s = sibling(zero)
    (other,) = after((other,), z_came)
    other_s = sibling(other)
    (input_grad,) = join((3,), (own, *z_came))
    weight_grad = finish(factor, zero, other, zero_s, other_s)
    return (activated, input_grad.T, weight_grad)


def solution(mesh):
    placed = (P(("depth", "row"), "col"), P("row", "col"), P(("depth", "row"), "col"))
    return jax.shard_map(
        shards,
        mesh=mesh,
        in_specs=placed,
        out_specs=(P(("depth", "row"), "col"), P(("depth", "row"), "col"), P("row", "col")),
        check_vma=False,
    )
```
